32 devices in a mesh: clips: 2 (over x), rows: 16 (over z, y, core).
Axes of the slice: x: 2, y: 2, z: 4, core: 2. Of those that a mesh axis runs over, the one named last changes fastest.
Arguments:
- latents: bfloat16 [8, 64, 160, 384], P('clips', 'rows'), parts along dimension 0, may hold values from -6 to 6
- gamma: float32 [384], replicated, may hold values from 0.5 to 1.5
- weight: bfloat16 [3, 3, 3, 384, 384], replicated, may hold values from -0.0625 to 0.0625
- bias: float32 [384], replicated, may hold values from -3 to 3
- intersection: int32 [32], P('clips'), parts along dimension 0, may hold values from 0 to 2
- ramp: int32 [32], P('clips'), parts along dimension 0, may hold values from 1 to 3
Outputs:
- decoded: bfloat16 [8, 64, 160, 384], P('clips', 'rows'), parts along dimension 0
The draws below stay inside these ranges and needn't reach their ends.
There are 2 independent parts, one for each index of `clips`. The reference program is written for one: setup_inputs(seed, part) draws one part's arguments, and reference() takes and returns one part's arrays. A program takes and returns all parts, laid end to end along the dimension named above; an argument that names none is the same for every part. Nothing has to cross between parts.
All inputs are finite; a program needn't handle non-finite values.
Results may differ from the reference program's by a relative error of at most 0.0034.
Values may be sent and summed in bfloat16 or wider, within the bound.
A program may use at most 448 MiB of HBM per device.

```python
import jax
import jax.numpy as jnp
from jax import lax

C = 384
W = 160
FRAMES = 4
ROWS_DEV = 4
OV_MAX = 2
TILES = 16
H = 64


def with_ends(values, stream_key, smallest, largest):
    shape = values.shape
    index_at = [jax.random.randint(jax.random.fold_in(stream_key, axis), (), 0, shape[axis]) for axis in range(len(shape))]
    values = values.at[tuple(index_at)].set(smallest)
    longest = shape.index(max(shape))
    index_at[longest] = (index_at[longest] + 1) % shape[longest]
    return values.at[tuple(index_at)].set(largest)


def block_scale(stream_key, shape, shards, low, largest):
    factor_of, own = 1.0, jax.random.fold_in(stream_key, 6)
    for position, parts in shards:
        heights = jnp.exp(jax.random.uniform(jax.random.fold_in(own, position), (parts,), jnp.float32, low / len(shards), largest / len(shards)))
        factor_of = factor_of * jnp.repeat(heights, shape[position] // parts).reshape([-1 if axis == position else 1 for axis in range(len(shape))])
    return factor_of


def scatter_about(rng, extent, scale, most, cuts=(), held_as=jnp.bfloat16):
    drawn = jax.random.normal(rng, extent, jnp.float32) * scale
    if len(cuts) > 0:
        drawn = block_scale(rng, extent, cuts, -0.22, 0.18) * drawn
    return jnp.clip(drawn, min=-most, max=most).astype(held_as)


def setup_inputs(seed: int = 0, part: int = 0) -> dict:
    splits = jax.random.split(jax.random.key(seed), 7)
    own_keys = jax.random.split(jax.random.fold_in(splits[6], part), 7)
    return {
        "latents": scatter_about(own_keys[0], (FRAMES, H, W, C), 1.0, 6.0, ((1, 16),)),
        "gamma": jnp.clip(jax.random.uniform(splits[1], (C,), jnp.float32, 0.5, 1.5), 0.5, 1.5),
        "weight": scatter_about(splits[2], (3, 3, 3, C, C), (27 * C) ** -0.5, 0.0625),
        "bias": scatter_about(splits[3], (C,), 0.5, 3.0, (), jnp.float32),
        "intersection": with_ends(jax.random.randint(own_keys[4], (TILES,), 0, OV_MAX + 1), jax.random.fold_in(own_keys[4], 1), 0, OV_MAX).astype(jnp.int32),
        "ramp": with_ends(jax.random.randint(own_keys[5], (TILES,), 1, 4), jax.random.fold_in(own_keys[5], 1), 1, 3).astype(jnp.int32),
    }


def activate(tile, gamma, keep):
    values = tile.astype(jnp.float32)
    square = lax.optimization_barrier(jnp.mean(values * values, axis=-1, keepdims=True))
    normed = values * lax.rsqrt(square + 1e-06) * gamma
    return (jax.nn.silu(normed) * keep).astype(jnp.bfloat16)

def convolve(stacked, weight, bias, count):
    padded = jnp.pad(stacked, ((0, 0), (1, 1), (1, 1), (0, 0)))
    height = stacked.shape[1]
    width = stacked.shape[2]
    total = jnp.zeros((count, height, width, weight.shape[4]), jnp.float32)
    for step_t in range(3):
        for step_h in range(3):
            for step_w in range(3):
                slab = padded[step_t:step_t + count, step_h:step_h + height, step_w:step_w + width]
                total = total + jnp.einsum('fhwc,cd->fhwd', slab, weight[step_t, step_h, step_w], preferred_element_type=jnp.float32)
    return total + bias

def decode_tile(tile, keep, gamma, weight, bias):
    act = activate(tile, gamma, keep)
    stacked = jnp.pad(act, ((2, 0), (0, 0), (0, 0), (0, 0)))
    return (tile.astype(jnp.float32) + convolve(stacked, weight, bias, tile.shape[0])).astype(jnp.bfloat16)

def reference(latents, gamma, weight, bias, intersection, ramp):
    rows = ROWS_DEV
    extra = OV_MAX
    tiles = TILES
    padded = jnp.pad(latents, ((0, 0), (0, extra), (0, 0), (0, 0)))
    numbers = jnp.arange(tiles, dtype=jnp.int32)
    eff = jnp.where(numbers == tiles - 1, 0, intersection).astype(jnp.int32)
    places = jnp.arange(rows + extra, dtype=jnp.int32)

    def one_tile(number):
        tile = lax.dynamic_slice_in_dim(padded, (number * rows).astype(jnp.int32), rows + extra, 1)
        keep = (places < rows + eff[number]).astype(jnp.float32).reshape(1, -1, 1, 1)
        return decode_tile(tile, keep, gamma, weight, bias)
    outs = lax.map(one_tile, numbers)
    own = outs[:, :, :rows]
    ext = outs[:, :, rows:]
    prev_ext = jnp.concatenate([jnp.zeros_like(ext[:1]), ext[:-1]], axis=0)
    prev_ov = jnp.concatenate([jnp.zeros((1,), jnp.int32), eff[:-1]], axis=0)
    prev_ramp = jnp.concatenate([jnp.zeros((1,), jnp.int32), ramp[:-1]], axis=0)
    offsets = jnp.arange(extra, dtype=jnp.int32)
    blend_w = jnp.where(offsets[None, :] < prev_ov[:, None], jnp.maximum(prev_ramp[:, None] - offsets[None, :], 0).astype(jnp.float32) / (prev_ramp[:, None] + 1).astype(jnp.float32), jnp.float32(0.0)).astype(jnp.float32)
    blend_w = blend_w.reshape(tiles, 1, extra, 1, 1)
    head = own[:, :, :extra].astype(jnp.float32)
    mixed = (blend_w * prev_ext.astype(jnp.float32) + (1.0 - blend_w) * head).astype(jnp.bfloat16)
    result = jnp.concatenate([mixed, own[:, :, extra:]], axis=2)
    result = jnp.transpose(result, (1, 0, 2, 3, 4))
    return result.reshape(result.shape[0], tiles * rows, result.shape[3], result.shape[4])
```

```python
import functools

import jax
import jax.numpy as jnp
from jax import lax
from jax.experimental import pallas as pl
from jax.experimental.pallas import tpu as pltpu
from jax.sharding import PartitionSpec as P

TAPS = 3
STEP = 256
MESH = pl.DeviceIdType.MESH

ROW_OF = ((1, 2), (0, 3))


def kernel(
    frames, width, chans, count,
    x_ref, w_ref, gamma_ref, bias_ref, inter_ref, ramp_ref,
    out_ref,
    xbuf, top, bot, lhs, wbuf, acc, ost,
    xsem, wsem, osem, send_sem, recv_sem,
):
    me = lax.axis_index("rows")
    span = TAPS * chans
    last = xbuf.shape[1] - 1

    def x_copy(f):
        return pltpu.make_async_copy(x_ref.at[f], xbuf.at[f], xsem.at[f])

    def w_copy(t):
        return pltpu.make_async_copy(
            w_ref.at[TAPS - 1 - t], wbuf.at[:, pl.ds(t * chans, chans)], wsem.at[t]
        )

    down = pltpu.make_async_remote_copy(
        src_ref=x_ref.at[:, last], dst_ref=top, send_sem=send_sem.at[0],
        recv_sem=recv_sem.at[0], device_id={"rows": me + 1}, device_id_type=MESH,
    )
    up = pltpu.make_async_remote_copy(
        src_ref=x_ref.at[:, 0], dst_ref=bot, send_sem=send_sem.at[1],
        recv_sem=recv_sem.at[1], device_id={"rows": me - 1}, device_id_type=MESH,
    )

    for f in range(frames):
        x_copy(f).start()
    for t in range(TAPS):
        w_copy(t).start()

    barrier = pltpu.get_barrier_semaphore()

    @pl.when(me > 0)
    def _():
        pl.semaphore_signal(
            barrier, inc=1, device_id={"rows": me - 1}, device_id_type=MESH
        )

    @pl.when(me < count - 1)
    def _():
        pl.semaphore_signal(
            barrier, inc=1, device_id={"rows": me + 1}, device_id_type=MESH
        )

    peers = jnp.where(me > 0, 1, 0) + jnp.where(me < count - 1, 1, 0)
    pl.semaphore_wait(barrier, peers)

    @pl.when(me < count - 1)
    def _():
        down.start()

    @pl.when(me > 0)
    def _():
        up.start()

    before = jnp.maximum(me - 1, 0)
    prev_ov = jnp.where(me > 0, inter_ref[before], 0)
    own_ov = jnp.where(me == count - 1, 0, inter_ref[me])
    ovv = jnp.full((1, chans), prev_ov, jnp.int32)
    ownv = jnp.full((1, chans), own_ov, jnp.int32)
    rampv = jnp.full((1, chans), ramp_ref[before], jnp.int32).astype(jnp.float32)
    a0 = jnp.where(ovv > 0, jnp.maximum(rampv, 0.0) / (rampv + 1.0), 0.0)
    a1 = jnp.where(ovv > 1, jnp.maximum(rampv - 1.0, 0.0) / (rampv + 1.0), 0.0)
    s1 = jnp.where(ovv > 1, 1.0, 1.0 - a0)
    s2 = 1.0 - a1
    live = jnp.where(ownv > 0, 1.0, 0.0)
    gamma = gamma_ref[...]
    bias = bias_ref[...]
    columns = lax.broadcasted_iota(jnp.int32, (width, chans), 0)

    def activate(values):
        square = jnp.mean(values * values, axis=-1, keepdims=True)
        half = values * lax.rsqrt(square + 1e-06) * (0.5 * gamma)
        return half + half * jnp.tanh(half)

    def place(f, value, targets):
        left = jnp.where(columns == 0, 0.0, pltpu.roll(value, 1, 0))
        right = jnp.where(columns == width - 1, 0.0, pltpu.roll(value, width - 1, 0))
        for scale, spots in targets:
            for step_w, part in enumerate((left, value, right)):
                if scale is not None:
                    part = part * scale
                part = part.astype(jnp.bfloat16)
                for half, slot, step_h in spots:
                    lhs[
                        half, f, slot * width : (slot + 1) * width,
                        step_h * span + step_w * chans : step_h * span + (step_w + 1) * chans,
                    ] = part

    own_targets = (
        ((None, ((1, 0, 1), (0, 0, 0))),),
        ((None, ((0, 0, 1), (0, 1, 0))), (s1, ((1, 0, 2),))),
        ((None, ((0, 1, 1), (1, 1, 0))), (s2, ((0, 0, 2),))),
        ((None, ((0, 1, 2), (1, 1, 1))),),
    )
    home = ((1, 0), (0, 0), (0, 1), (1, 1))

    wbuf[:, TAPS * chans :] = jnp.zeros(
        (wbuf.shape[0], wbuf.shape[1] - TAPS * chans), wbuf.dtype
    )
    acc[:, :, frames * chans :] = jnp.zeros(
        (2, 2 * width, acc.shape[2] - frames * chans), acc.dtype
    )

    def own_frame(f, carry):
        x_copy(f).wait()
        at = pl.ds(pl.multiple_of(f * chans, 128), chans)
        for row in range(last + 1):
            values = xbuf[f, row].astype(jnp.float32)
            half, slot = home[row]
            acc[half, slot * width : (slot + 1) * width, at] = values + bias
            place(f, activate(values), own_targets[row])
        return carry

    lax.fori_loop(0, frames, own_frame, 0)

    def multiply(half, f, j):
        taken = pl.ds(pl.multiple_of(j * STEP, STEP), STEP)
        put = pl.ds(pl.multiple_of(f * chans + j * STEP, 128), STEP)
        acc[half, :, put] += jnp.dot(
            lhs[half, f], wbuf[:, taken], preferred_element_type=jnp.float32
        )

    def out_copy(half, f, slot):
        row = ROW_OF[half][slot]
        return pltpu.make_async_copy(
            ost.at[f, row], out_ref.at[f, row], osem.at[f, row]
        )

    def work(half):
        for f in range(frames):
            reach = min(TAPS, frames - f) * chans
            steps = -(-reach // STEP)

            def body(j, carry, f=f):
                multiply(half, f, j)
                return carry

            lax.fori_loop(0, steps, body, 0)
            for slot in range(2):
                ost[f, ROW_OF[half][slot]] = acc[
                    half, slot * width : (slot + 1) * width, f * chans : (f + 1) * chans
                ].astype(jnp.bfloat16)
                out_copy(half, f, slot).start()

    for t in range(TAPS):
        w_copy(t).wait()
    work(0)

    @pl.when(me > 0)
    def _():
        down.wait_recv()

    @pl.when(me == 0)
    def _():
        top[...] = jnp.zeros(top.shape, top.dtype)

    @pl.when(me < count - 1)
    def _():
        up.wait_recv()

    @pl.when(me == count - 1)
    def _():
        bot[...] = jnp.zeros(bot.shape, bot.dtype)

    def edge_frame(f, carry):
        place(f, activate(top[f].astype(jnp.float32)), ((a0, ((1, 0, 0),)),))
        place(f, activate(bot[f].astype(jnp.float32)), ((live, ((1, 1, 2),)),))
        return carry

    lax.fori_loop(0, frames, edge_frame, 0)
    work(1)

    for half in range(2):
        for f in range(frames):
            for slot in range(2):
                out_copy(half, f, slot).wait()

    @pl.when(me < count - 1)
    def _():
        down.wait_send()

    @pl.when(me > 0)
    def _():
        up.wait_send()


def per_device(latents, gamma, weight, bias, intersection, ramp):
    frames, rows, width, chans = latents.shape
    count = lax.axis_size("rows")
    taps = weight.reshape(TAPS, TAPS * TAPS * chans, chans)
    depth = taps.shape[1]
    wide = -(-TAPS * chans // STEP) * STEP
    total = (frames - 1) * chans + -(-chans // STEP) * STEP
    total = max(total, (frames - TAPS) * chans + wide)
    any_space = pl.BlockSpec(memory_space=pl.ANY)
    vmem = pl.BlockSpec(memory_space=pltpu.VMEM)
    smem = pl.BlockSpec(memory_space=pltpu.SMEM)
    return pl.pallas_call(
        functools.partial(kernel, frames, width, chans, count),
        out_shape=jax.ShapeDtypeStruct(latents.shape, latents.dtype),
        in_specs=[any_space, any_space, vmem, vmem, smem, smem],
        out_specs=any_space,
        scratch_shapes=[
            pltpu.VMEM((frames, rows, width, chans), jnp.bfloat16),
            pltpu.VMEM((frames, width, chans), jnp.bfloat16),
            pltpu.VMEM((frames, width, chans), jnp.bfloat16),
            pltpu.VMEM((2, frames, 2 * width, depth), jnp.bfloat16),
            pltpu.VMEM((depth, wide), jnp.bfloat16),
            pltpu.VMEM((2, 2 * width, total), jnp.float32),
            pltpu.VMEM((frames, rows, width, chans), jnp.bfloat16),
            pltpu.SemaphoreType.DMA((frames,)),
            pltpu.SemaphoreType.DMA((TAPS,)),
            pltpu.SemaphoreType.DMA((frames, rows)),
            pltpu.SemaphoreType.DMA((2,)),
            pltpu.SemaphoreType.DMA((2,)),
        ],
        compiler_params=pltpu.CompilerParams(
            collective_id=0, has_side_effects=True, vmem_limit_bytes=50 * 1024 * 1024
        ),
    )(latents, taps, gamma.reshape(1, chans), bias.reshape(1, chans), intersection, ramp)


def solution(mesh):
    in_specs = (P("clips", "rows", None, None), P(), P(), P(), P("clips"), P("clips"))
    out_specs = P("clips", "rows", None, None)
    return jax.shard_map(
        per_device, mesh=mesh, in_specs=in_specs, out_specs=out_specs, check_vma=False
    )
```

```python
import functools

import jax
import jax.numpy as jnp
from jax import lax
from jax.experimental import pallas as pl
from jax.experimental.pallas import tpu as pltpu
from jax.sharding import PartitionSpec as P

TAPS = 3
MESH = pl.DeviceIdType.MESH

ROW_OF = ((1, 2), (0, 3))


def kernel(
    frames, width, chans, count,
    x_ref, w_ref, gamma_ref, bias_ref, inter_hbm, ramp_hbm,
    out_ref,
    xbuf, top, bot, lhs, wbuf, acc, ost, inter_ref, ramp_ref,
    xsem, wsem, osem, ssem, send_sem, recv_sem,
):
    me = lax.axis_index("rows")
    span = TAPS * chans
    last = xbuf.shape[1] - 1

    def x_copy(f):
        return pltpu.make_async_copy(x_ref.at[f], xbuf.at[f], xsem.at[f])

    def w_copy(t):
        return pltpu.make_async_copy(
            w_ref.at[TAPS - 1 - t], wbuf.at[:, pl.ds(t * chans, chans)], wsem.at[t]
        )

    down = pltpu.make_async_remote_copy(
        src_ref=x_ref.at[:, last], dst_ref=top, send_sem=send_sem.at[0],
        recv_sem=recv_sem.at[0], device_id={"rows": me + 1}, device_id_type=MESH,
    )
    up = pltpu.make_async_remote_copy(
        src_ref=x_ref.at[:, 0], dst_ref=bot, send_sem=send_sem.at[1],
        recv_sem=recv_sem.at[1], device_id={"rows": me - 1}, device_id_type=MESH,
    )

    small = (
        pltpu.make_async_copy(inter_hbm, inter_ref, ssem.at[0]),
        pltpu.make_async_copy(ramp_hbm, ramp_ref, ssem.at[1]),
    )
    for copy in small:
        copy.start()
    for f in range(frames):
        x_copy(f).start()
    for t in range(TAPS):
        w_copy(t).start()

    barrier = pltpu.get_barrier_semaphore()

    @pl.when(me > 0)
    def _():
        pl.semaphore_signal(
            barrier, inc=1, device_id={"rows": me - 1}, device_id_type=MESH
        )

    @pl.when(me < count - 1)
    def _():
        pl.semaphore_signal(
            barrier, inc=1, device_id={"rows": me + 1}, device_id_type=MESH
        )

    peers = jnp.where(me > 0, 1, 0) + jnp.where(me < count - 1, 1, 0)
    pl.semaphore_wait(barrier, peers)

    @pl.when(me < count - 1)
    def _():
        down.start()

    @pl.when(me > 0)
    def _():
        up.start()

    for copy in small:
        copy.wait()

    before = jnp.maximum(me - 1, 0)
    prev_ov = jnp.where(me > 0, inter_ref[before], 0)
    own_ov = jnp.where(me == count - 1, 0, inter_ref[me])
    ovv = jnp.full((1, chans), prev_ov, jnp.int32)
    ownv = jnp.full((1, chans), own_ov, jnp.int32)
    rampv = jnp.full((1, chans), ramp_ref[before], jnp.int32).astype(jnp.float32)
    a0 = jnp.where(ovv > 0, jnp.maximum(rampv, 0.0) / (rampv + 1.0), 0.0)
    a1 = jnp.where(ovv > 1, jnp.maximum(rampv - 1.0, 0.0) / (rampv + 1.0), 0.0)
    s1 = jnp.where(ovv > 1, 1.0, 1.0 - a0)
    s2 = 1.0 - a1
    live = jnp.where(ownv > 0, 1.0, 0.0)
    gamma = gamma_ref[...].reshape(1, chans)
    bias = bias_ref[...].reshape(1, chans)
    columns = lax.broadcasted_iota(jnp.int32, (width, chans), 0)

    def activate(values):
        square = jnp.mean(values * values, axis=-1, keepdims=True)
        half = values * lax.rsqrt(square + 1e-06) * (0.5 * gamma)
        return half + half * jnp.tanh(half)

    def place(f, value, targets):
        left = jnp.where(columns == 0, 0.0, pltpu.roll(value, 1, 0))
        right = jnp.where(columns == width - 1, 0.0, pltpu.roll(value, width - 1, 0))
        for scale, spots in targets:
            for step_w, part in enumerate((left, value, right)):
                if scale is not None:
                    part = part * scale
                part = part.astype(jnp.bfloat16)
                for half, slot, step_h in spots:
                    lhs[
                        half, f, slot * width : (slot + 1) * width,
                        step_h * span + step_w * chans : step_h * span + (step_w + 1) * chans,
                    ] = part

    own_targets = (
        ((None, ((1, 0, 1), (0, 0, 0))),),
        ((None, ((0, 0, 1), (0, 1, 0))), (s1, ((1, 0, 2),))),
        ((None, ((0, 1, 1), (1, 1, 0))), (s2, ((0, 0, 2),))),
        ((None, ((0, 1, 2), (1, 1, 1))),),
    )
    home = ((1, 0), (0, 0), (0, 1), (1, 1))

    def own_frame(f, carry):
        x_copy(f).wait()
        for row in range(last + 1):
            values = xbuf[f, row].astype(jnp.float32)
            half, slot = home[row]
            acc[half, f, slot * width : (slot + 1) * width] = values + bias
            place(f, activate(values), own_targets[row])
        return carry

    lax.fori_loop(0, frames, own_frame, 0)

    def multiply(half, start, stop, t0, t1):
        block = lhs[half, start:stop].reshape((stop - start) * 2 * width, TAPS * span)
        product = jnp.dot(
            block, wbuf[:, t0 * chans : t1 * chans], preferred_element_type=jnp.float32
        )
        for f in range(start, stop):
            for t in range(t0, t1):
                acc[half, f + t] += product[
                    (f - start) * 2 * width : (f - start + 1) * 2 * width,
                    (t - t0) * chans : (t - t0 + 1) * chans,
                ]

    def out_copy(half, f, slot):
        row = ROW_OF[half][slot]
        return pltpu.make_async_copy(
            ost.at[f, row], out_ref.at[f, row], osem.at[f, row]
        )

    def finish(half, start, stop):
        for f in range(start, stop):
            for slot in range(2):
                ost[f, ROW_OF[half][slot]] = acc[
                    half, f, slot * width : (slot + 1) * width
                ].astype(jnp.bfloat16)
                out_copy(half, f, slot).start()

    def work(half):
        multiply(half, 0, frames - 1, 0, 2)
        finish(half, 0, frames - 2)
        multiply(half, 0, frames - 2, 2, 3)
        finish(half, frames - 2, frames - 1)
        multiply(half, frames - 1, frames, 0, 1)
        finish(half, frames - 1, frames)

    for t in range(TAPS):
        w_copy(t).wait()
    work(0)

    @pl.when(me > 0)
    def _():
        down.wait_recv()

    @pl.when(me == 0)
    def _():
        top[...] = jnp.zeros(top.shape, top.dtype)

    @pl.when(me < count - 1)
    def _():
        up.wait_recv()

    @pl.when(me == count - 1)
    def _():
        bot[...] = jnp.zeros(bot.shape, bot.dtype)

    def edge_frame(f, carry):
        place(f, activate(top[f].astype(jnp.float32)), ((a0, ((1, 0, 0),)),))
        place(f, activate(bot[f].astype(jnp.float32)), ((live, ((1, 1, 2),)),))
        return carry

    lax.fori_loop(0, frames, edge_frame, 0)
    work(1)

    for half in range(2):
        for f in range(frames):
            for slot in range(2):
                out_copy(half, f, slot).wait()

    @pl.when(me < count - 1)
    def _():
        down.wait_send()

    @pl.when(me > 0)
    def _():
        up.wait_send()


def per_device(latents, gamma, weight, bias, intersection, ramp):
    frames, rows, width, chans = latents.shape
    count = lax.axis_size("rows")
    taps = weight.reshape(TAPS, TAPS * TAPS * chans, chans)
    depth = taps.shape[1]
    hbm = pl.BlockSpec(memory_space=pltpu.HBM)
    vmem = pl.BlockSpec(memory_space=pltpu.VMEM)
    return pl.pallas_call(
        functools.partial(kernel, frames, width, chans, count),
        out_shape=jax.ShapeDtypeStruct(latents.shape, latents.dtype),
        in_specs=[hbm, hbm, vmem, vmem, hbm, hbm],
        out_specs=hbm,
        scratch_shapes=[
            pltpu.VMEM((frames, rows, width, chans), jnp.bfloat16),
            pltpu.VMEM((frames, width, chans), jnp.bfloat16),
            pltpu.VMEM((frames, width, chans), jnp.bfloat16),
            pltpu.VMEM((2, frames, 2 * width, depth), jnp.bfloat16),
            pltpu.VMEM((depth, TAPS * chans), jnp.bfloat16),
            pltpu.VMEM((2, frames, 2 * width, chans), jnp.float32),
            pltpu.VMEM((frames, rows, width, chans), jnp.bfloat16),
            pltpu.SMEM(intersection.shape, jnp.int32),
            pltpu.SMEM(ramp.shape, jnp.int32),
            pltpu.SemaphoreType.DMA((frames,)),
            pltpu.SemaphoreType.DMA((TAPS,)),
            pltpu.SemaphoreType.DMA((frames, rows)),
            pltpu.SemaphoreType.DMA((2,)),
            pltpu.SemaphoreType.DMA((2,)),
            pltpu.SemaphoreType.DMA((2,)),
        ],
        compiler_params=pltpu.CompilerParams(
            collective_id=0, has_side_effects=True, vmem_limit_bytes=64 * 1024 * 1024
        ),
    )(latents, taps, gamma, bias, intersection, ramp)


def solution(mesh):
    in_specs = (P("clips", "rows", None, None), P(), P(), P(), P("clips"), P("clips"))
    out_specs = P("clips", "rows", None, None)
    return jax.shard_map(
        per_device, mesh=mesh, in_specs=in_specs, out_specs=out_specs, check_vma=False
    )
```

```python
import functools

import jax
import jax.numpy as jnp
from jax import lax
from jax.experimental import pallas as pl
from jax.experimental.pallas import tpu as pltpu
from jax.sharding import PartitionSpec as P

TAPS = 3
MESH = pl.DeviceIdType.MESH

ROW_OF = ((1, 2), (0, 3))


def kernel(
    frames, width, chans, count,
    x_ref, w_ref, gamma_ref, bias_ref, inter_hbm, ramp_hbm,
    out_ref,
    xbuf, top, bot, lhs, wbuf, acc, ost, inter_ref, ramp_ref,
    xsem, wsem, osem, ssem, send_sem, recv_sem,
):
    me = lax.axis_index("rows")
    span = TAPS * chans
    last = xbuf.shape[1] - 1

    def x_copy(f):
        return pltpu.make_async_copy(x_ref.at[f], xbuf.at[f], xsem.at[f])

    def w_copy(t):
        return pltpu.make_async_copy(
            w_ref.at[TAPS - 1 - t], wbuf.at[:, pl.ds(t * chans, chans)], wsem.at[t]
        )

    down = pltpu.make_async_remote_copy(
        src_ref=x_ref.at[:, last], dst_ref=top, send_sem=send_sem.at[0],
        recv_sem=recv_sem.at[0], device_id={"rows": me + 1}, device_id_type=MESH,
    )
    up = pltpu.make_async_remote_copy(
        src_ref=x_ref.at[:, 0], dst_ref=bot, send_sem=send_sem.at[1],
        recv_sem=recv_sem.at[1], device_id={"rows": me - 1}, device_id_type=MESH,
    )

    small = (
        pltpu.make_async_copy(inter_hbm, inter_ref, ssem.at[0]),
        pltpu.make_async_copy(ramp_hbm, ramp_ref, ssem.at[1]),
    )
    for copy in small:
        copy.start()
    for f in range(frames):
        x_copy(f).start()
    for t in range(TAPS):
        w_copy(t).start()

    barrier = pltpu.get_barrier_semaphore()

    @pl.when(me > 0)
    def _():
        pl.semaphore_signal(
            barrier, inc=1, device_id={"rows": me - 1}, device_id_type=MESH
        )

    @pl.when(me < count - 1)
    def _():
        pl.semaphore_signal(
            barrier, inc=1, device_id={"rows": me + 1}, device_id_type=MESH
        )

    peers = jnp.where(me > 0, 1, 0) + jnp.where(me < count - 1, 1, 0)
    pl.semaphore_wait(barrier, peers)

    @pl.when(me < count - 1)
    def _():
        down.start()

    @pl.when(me > 0)
    def _():
        up.start()

    for copy in small:
        copy.wait()

    before = jnp.maximum(me - 1, 0)
    prev_ov = jnp.where(me > 0, inter_ref[before], 0)
    own_ov = jnp.where(me == count - 1, 0, inter_ref[me])
    ovv = jnp.full((1, chans), prev_ov, jnp.int32)
    ownv = jnp.full((1, chans), own_ov, jnp.int32)
    rampv = jnp.full((1, chans), ramp_ref[before], jnp.int32).astype(jnp.float32)
    a0 = jnp.where(ovv > 0, jnp.maximum(rampv, 0.0) / (rampv + 1.0), 0.0)
    a1 = jnp.where(ovv > 1, jnp.maximum(rampv - 1.0, 0.0) / (rampv + 1.0), 0.0)
    s1 = jnp.where(ovv > 1, 1.0, 1.0 - a0)
    s2 = 1.0 - a1
    live = jnp.where(ownv > 0, 1.0, 0.0)
    gamma = gamma_ref[...].reshape(1, chans)
    bias = bias_ref[...].reshape(1, chans)
    columns = lax.broadcasted_iota(jnp.int32, (width, chans), 0)

    def activate(values):
        square = jnp.mean(values * values, axis=-1, keepdims=True)
        half = values * lax.rsqrt(square + 1e-06) * (0.5 * gamma)
        return half + half * jnp.tanh(half)

    def place(f, value, targets):
        left = jnp.where(columns == 0, 0.0, pltpu.roll(value, 1, 0))
        right = jnp.where(columns == width - 1, 0.0, pltpu.roll(value, width - 1, 0))
        for scale, spots in targets:
            for step_w, part in enumerate((left, value, right)):
                if scale is not None:
                    part = part * scale
                part = part.astype(jnp.bfloat16)
                for half, slot, step_h in spots:
                    lhs[
                        half, f, slot * width : (slot + 1) * width,
                        step_h * span + step_w * chans : step_h * span + (step_w + 1) * chans,
                    ] = part

    own_targets = (
        ((None, ((1, 0, 1), (0, 0, 0))),),
        ((None, ((0, 0, 1), (0, 1, 0))), (s1, ((1, 0, 2),))),
        ((None, ((0, 1, 1), (1, 1, 0))), (s2, ((0, 0, 2),))),
        ((None, ((0, 1, 2), (1, 1, 1))),),
    )

    def own_frame(f, carry):
        x_copy(f).wait()
        for row in range(last + 1):
            values = xbuf[f, row].astype(jnp.float32)
            place(f, activate(values), own_targets[row])
        return carry

    lax.fori_loop(0, frames, own_frame, 0)

    written = set()

    def multiply(half, start, stop, t0, t1):
        block = lhs[half, start:stop].reshape((stop - start) * 2 * width, TAPS * span)
        product = jnp.dot(
            block, wbuf[:, t0 * chans : t1 * chans], preferred_element_type=jnp.float32
        )
        for f in range(start, stop):
            for t in range(t0, t1):
                part = product[
                    (f - start) * 2 * width : (f - start + 1) * 2 * width,
                    (t - t0) * chans : (t - t0 + 1) * chans,
                ]
                if (half, f + t) in written:
                    acc[half, f + t] += part
                else:
                    acc[half, f + t] = part
                    written.add((half, f + t))

    def out_copy(half, f, slot):
        row = ROW_OF[half][slot]
        return pltpu.make_async_copy(
            ost.at[f, row], out_ref.at[f, row], osem.at[f, row]
        )

    def finish(half, start, stop):
        for f in range(start, stop):
            for slot in range(2):
                row = ROW_OF[half][slot]
                total = acc[half, f, slot * width : (slot + 1) * width]
                total = total + (xbuf[f, row].astype(jnp.float32) + bias)
                ost[f, row] = total.astype(jnp.bfloat16)
                out_copy(half, f, slot).start()

    def work(half):
        multiply(half, 0, frames - 1, 0, 2)
        finish(half, 0, frames - 2)
        multiply(half, 0, frames - 2, 2, 3)
        finish(half, frames - 2, frames - 1)
        multiply(half, frames - 1, frames, 0, 1)
        finish(half, frames - 1, frames)

    for t in range(TAPS):
        w_copy(t).wait()
    work(0)

    @pl.when(me > 0)
    def _():
        down.wait_recv()

    @pl.when(me == 0)
    def _():
        top[...] = jnp.zeros(top.shape, top.dtype)

    @pl.when(me < count - 1)
    def _():
        up.wait_recv()

    @pl.when(me == count - 1)
    def _():
        bot[...] = jnp.zeros(bot.shape, bot.dtype)

    def edge_frame(f, carry):
        place(f, activate(top[f].astype(jnp.float32)), ((a0, ((1, 0, 0),)),))
        place(f, activate(bot[f].astype(jnp.float32)), ((live, ((1, 1, 2),)),))
        return carry

    lax.fori_loop(0, frames, edge_frame, 0)
    work(1)

    for half in range(2):
        for f in range(frames):
            for slot in range(2):
                out_copy(half, f, slot).wait()

    @pl.when(me < count - 1)
    def _():
        down.wait_send()

    @pl.when(me > 0)
    def _():
        up.wait_send()


def hand_on(frames, rows, from_ref, to_ref, held, in_sem, out_sem):
    blocks = [(f, r) for f in range(frames) for r in range(rows)]
    fetch = [
        pltpu.make_async_copy(from_ref.at[at], held.at[at], in_sem.at[at])
        for at in blocks
    ]
    store = [
        pltpu.make_async_copy(held.at[at], to_ref.at[at], out_sem.at[at])
        for at in blocks
    ]
    for copy in fetch:
        copy.start()
    for arriving, leaving in zip(fetch, store):
        arriving.wait()
        leaving.start()
    for copy in store:
        copy.wait()


def per_device(latents, gamma, weight, bias, intersection, ramp):
    frames, rows, width, chans = latents.shape
    count = lax.axis_size("rows")
    taps = weight.reshape(TAPS, TAPS * TAPS * chans, chans)
    depth = taps.shape[1]
    hbm = pl.BlockSpec(memory_space=pltpu.HBM)
    vmem = pl.BlockSpec(memory_space=pltpu.VMEM)
    made = pl.pallas_call(
        functools.partial(kernel, frames, width, chans, count),
        out_shape=jax.ShapeDtypeStruct(latents.shape, latents.dtype),
        in_specs=[hbm, hbm, vmem, vmem, hbm, hbm],
        out_specs=hbm,
        scratch_shapes=[
            pltpu.VMEM((frames, rows, width, chans), jnp.bfloat16),
            pltpu.VMEM((frames, width, chans), jnp.bfloat16),
            pltpu.VMEM((frames, width, chans), jnp.bfloat16),
            pltpu.VMEM((2, frames, 2 * width, depth), jnp.bfloat16),
            pltpu.VMEM((depth, TAPS * chans), jnp.bfloat16),
            pltpu.VMEM((2, frames, 2 * width, chans), jnp.float32),
            pltpu.VMEM((frames, rows, width, chans), jnp.bfloat16),
            pltpu.SMEM(intersection.shape, jnp.int32),
            pltpu.SMEM(ramp.shape, jnp.int32),
            pltpu.SemaphoreType.DMA((frames,)),
            pltpu.SemaphoreType.DMA((TAPS,)),
            pltpu.SemaphoreType.DMA((frames, rows)),
            pltpu.SemaphoreType.DMA((2,)),
            pltpu.SemaphoreType.DMA((2,)),
            pltpu.SemaphoreType.DMA((2,)),
        ],
        compiler_params=pltpu.CompilerParams(
            collective_id=0, has_side_effects=True, vmem_limit_bytes=64 * 1024 * 1024
        ),
    )(latents, taps, gamma, bias, intersection, ramp)
    return pl.pallas_call(
        functools.partial(hand_on, frames, rows),
        out_shape=jax.ShapeDtypeStruct(latents.shape, latents.dtype),
        in_specs=[hbm],
        out_specs=hbm,
        scratch_shapes=[
            pltpu.VMEM((frames, rows, width, chans), jnp.bfloat16),
            pltpu.SemaphoreType.DMA((frames, rows)),
            pltpu.SemaphoreType.DMA((frames, rows)),
        ],
        compiler_params=pltpu.CompilerParams(vmem_limit_bytes=64 * 1024 * 1024),
    )(made)


def solution(mesh):
    in_specs = (P("clips", "rows", None, None), P(), P(), P(), P("clips"), P("clips"))
    out_specs = P("clips", "rows", None, None)
    return jax.shard_map(
        per_device, mesh=mesh, in_specs=in_specs, out_specs=out_specs, check_vma=False
    )
```
